128 devices in a mesh: ta: 2 (over core), ha: 8 (over x_lo, z), wa: 8 (over y, x_hi).
Axes of the slice: x: 4 (x_hi: 2, x_lo: 2; x = x_hi * 2 + x_lo), y: 4, z: 4, core: 2. Of those that a mesh axis runs over, the one named last changes fastest.
Arguments:
- queries: bfloat16 [48, 64, 64, 256], P(('ta', 'ha'), None, 'wa'), may hold values from -100 to 100
- key_field: bfloat16 [48, 64, 64, 256], P(('ta', 'ha'), None, 'wa'), may hold values from -4.1 to 4.1
- value_field: bfloat16 [48, 64, 64, 256], P(('ta', 'ha'), None, 'wa'), may hold values from -6 to 6
Outputs:
- attended: bfloat16 [48, 64, 64, 256], P(('ta', 'ha'), None, 'wa')
The draws below stay inside these ranges and needn't reach their ends.
All inputs are finite; a program needn't handle non-finite values.
Results may differ from the reference program's by a relative error of at most 0.0048.
Values may be sent and summed in bfloat16 or wider, within the bound.
A program may use at most 128 MiB of HBM per device.

```python
import jax
import jax.numpy as jnp
from jax import lax

HEAD = 128
HEADS = 2
TT = 6
TH = 8
TW = 8
FRAMES = 48
HEIGHT = 64
WIDTH = 64


def draw_queries(key, part):
    key = jax.random.fold_in(key, 7)
    first_key = jax.random.fold_in(key, 0)
    shape = (FRAMES, HEIGHT, WIDTH, HEADS * HEAD)
    result = jnp.clip(jax.random.normal(first_key, shape, jnp.float32), -4.0, 4.0)
    return result.astype(jnp.bfloat16)


def draw_key_field(key, part):
    key = jax.random.fold_in(key, 11)
    shape = (FRAMES, HEIGHT, WIDTH, HEADS * HEAD)
    result = jnp.clip(jax.random.normal(key, shape, jnp.float32), -4.0, 4.0)
    return result.astype(jnp.bfloat16)


def level_of(rng, shape, cuts, smallest, high):
    loudness, own = 1.0, jax.random.fold_in(rng, 6)
    for axis_at, shards_of in cuts:
        steps = jnp.exp(jax.random.uniform(jax.random.fold_in(own, axis_at), (shards_of,), jnp.float32, smallest / len(cuts), high / len(cuts)))
        loudness = loudness * jnp.repeat(steps, shape[axis_at] // shards_of).reshape([-1 if axis == axis_at else 1 for axis in range(len(shape))])
    return loudness


def noise(own_key, shape, deviation, bound, cuts=(), kind=jnp.bfloat16):
    array = deviation * jax.random.normal(own_key, shape, jnp.float32)
    if cuts:
        array = array * level_of(own_key, shape, cuts, -0.22, 0.18)
    return jnp.clip(array, -bound, bound).astype(kind)


def setup_inputs(seed: int = 0) -> dict:
    key_of = jax.random.split(jax.random.key(seed), 4)
    queries = draw_queries(jax.random.fold_in(key_of[3], 71), 0)
    key_field = draw_key_field(jax.random.fold_in(key_of[3], 71), 0)
    value_field = noise(key_of[2], (FRAMES, HEIGHT, WIDTH, HEADS * HEAD), 1.0, 6.0, ((0, 16), (2, 8)))
    return {"queries": queries, "key_field": key_field, "value_field": value_field}


def head_attention(query_part, key_part, value_part, allowed):
    scores = jnp.dot(query_part, key_part.T, preferred_element_type=jnp.float32) * (query_part.shape[1] ** -0.5)
    scores = jnp.where(allowed[None, :], scores, -jnp.inf)
    largest = jnp.max(scores, axis=1, keepdims=True)
    expon = jnp.exp(scores - largest)
    totals = jnp.sum(expon, axis=1, keepdims=True)
    weights = expon.astype(jnp.bfloat16)
    summed = jnp.dot(weights, value_part, preferred_element_type=jnp.float32)
    return (summed / totals).astype(jnp.bfloat16)


def reference(queries, key_field, value_field):
    frames, height, width, channels = queries.shape
    tile_len = TT * TH * TW
    grid_t = frames // TT
    grid_h = height // TH
    grid_w = width // TW

    def tiled(field):
        shaped = field.reshape(grid_t, TT, grid_h, TH, grid_w, TW, channels)
        return shaped.transpose(0, 2, 4, 1, 3, 5, 6).reshape(grid_t, grid_h, grid_w, tile_len, channels)

    margins = ((1, 1), (1, 1), (1, 1), (0, 0), (0, 0))
    query_tiles = tiled(queries)
    key_tiles = jnp.pad(tiled(key_field), margins)
    value_tiles = jnp.pad(tiled(value_field), margins)
    present = jnp.pad(jnp.ones((grid_t, grid_h, grid_w), dtype=bool), 1)

    def attend_tile(tile_flat):
        t_idx = (tile_flat // (grid_h * grid_w)).astype(jnp.int32)
        h_idx = ((tile_flat // grid_w) % grid_h).astype(jnp.int32)
        w_idx = (tile_flat % grid_w).astype(jnp.int32)
        anchor = jnp.zeros((), jnp.int32)
        start = (t_idx, h_idx, w_idx, anchor, anchor)
        key_win = lax.dynamic_slice(key_tiles, start, (3, 3, 3, tile_len, channels)).reshape(27 * tile_len, channels)
        value_win = lax.dynamic_slice(value_tiles, start, (3, 3, 3, tile_len, channels)).reshape(27 * tile_len, channels)
        allowed = jnp.repeat(lax.dynamic_slice(present, (t_idx, h_idx, w_idx), (3, 3, 3)).reshape(27), tile_len)
        query_rows = query_tiles[t_idx, h_idx, w_idx]
        outputs = []
        for head_num in range(HEADS):
            offset = head_num * HEAD
            outputs.append(head_attention(query_rows[:, offset:offset + HEAD], key_win[:, offset:offset + HEAD], value_win[:, offset:offset + HEAD], allowed))
        return jnp.concatenate(outputs, axis=1)

    blocks = lax.map(attend_tile, jnp.arange(grid_t * grid_h * grid_w, dtype=jnp.int32))
    shaped = blocks.reshape(grid_t, grid_h, grid_w, TT, TH, TW, channels)
    return shaped.transpose(0, 3, 1, 4, 2, 5, 6).reshape(frames, height, width, channels)
```

```python
import functools

import jax
import jax.numpy as jnp
from jax import lax
from jax.experimental import pallas as pl
from jax.experimental.pallas import tpu as pltpu
from jax.sharding import PartitionSpec as P

HEAD = 128
HEADS = 2
ROWS = 8
FR = 3
LINE = 64
TOK = FR * LINE
FACTOR = HEAD**-0.5 * 1.4426950408889634
MESH = pl.DeviceIdType.MESH
BF = jnp.bfloat16
F32 = jnp.float32

A, D, E, B, C, F = range(6)
STREAMS = ("kr", "kl", "vr", "vl", "kf", "vf", "qb", "qc", "qd0", "qd1", "qe", "qf")
RETURNS = {B: 0, C: 1, D: 2, E: 3, F: 4}
LOCAL = {A: 0, D: 1, C: 2}


def rows_of(chunk):
    return pl.ds(pl.multiple_of(chunk * LINE, LINE), LINE)


def inside(chunk):
    return (chunk >= 0) & (chunk < ROWS)


def merge(parts):
    top = functools.reduce(jnp.maximum, [log for _, log in parts])
    shares = [jnp.exp2(log - top) for _, log in parts]
    total = functools.reduce(jnp.add, shares)
    value = functools.reduce(jnp.add, [share * out for share, (out, _) in zip(shares, parts)])
    return value / total, top + jnp.log2(total)


def kernel(
    q_in, k_in, v_in, out, kbuf, vbuf, qbuf, okeep, lkeep, osend, lsend, orecv, lrecv, local_sem, send_sem, recv_sem,
    osend_sem, orecv_sem, lsend_sem, lrecv_sem
):
    core = lax.axis_index("ta")
    ha = lax.axis_index("ha")
    wa = lax.axis_index("wa")
    z, x_lo, y, x_hi = ha % 4, ha // 4, wa // 2, wa % 2
    zt = z // 2

    def device(lo, hi, yy, zz, cc):
        return {"ta": cc, "ha": lo * 4 + zz, "wa": yy * 2 + hi}

    swap = 1 - (x_lo + zt) % 2
    out_core = (core + swap) % 2
    in_core = (core + 1 - swap) % 2
    has_other = (swap == 1) | (core == zt)
    sends_other = (swap == 0) | (core != zt)
    right = device(x_lo, x_hi, y, (z + 1) % 4, core)
    left = device(x_lo, x_hi, y, (z + 3) % 4, core)
    step_y = 1 - 2 * x_hi
    y_next = device(x_lo, x_hi, (y + step_y + 4) % 4, z, core)
    y_prev = device(x_lo, x_hi, (y - step_y + 4) % 4, z, core)
    y_first = 3 * x_hi
    has_prev = y != y_first
    has_next = y != 3 - y_first
    near_out = device(1 - x_lo, x_hi, y, z, out_core)
    near_in = device(1 - x_lo, x_hi, y, z, in_core)
    diag_out = device(1 - x_lo, 1 - x_hi, y, z, out_core)
    diag_in = device(1 - x_lo, 1 - x_hi, y, z, in_core)
    across = device(x_lo, 1 - x_hi, y, z, core)

    barrier = pltpu.get_barrier_semaphore()
    peers = (right, left, y_next, y_prev, near_out, near_in, diag_out, diag_in, across)
    for peer in peers:
        pl.semaphore_signal(barrier, inc=1, device_id=peer, device_id_type=MESH)
    pl.semaphore_wait(barrier, len(peers))

    def remote(stream, chunk, src, dst, target):
        at = STREAMS.index(stream)
        return pltpu.make_async_remote_copy(
            src_ref=src, dst_ref=dst, send_sem=send_sem.at[at, chunk], recv_sem=recv_sem.at[at, chunk],
            device_id=target, device_id_type=MESH
        )

    def part(ref, *lead, chunk, lanes=pl.ds(0, 2 * HEAD)):
        return ref.at[(*lead, slice(None), rows_of(chunk), lanes)]

    first, second = pl.ds(0, HEAD), pl.ds(HEAD, HEAD)

    def copy(stream, chunk):
        if stream in ("kr", "kl"):
            return remote(stream, chunk, part(k_in, chunk=chunk), part(kbuf, z, chunk=chunk), right if stream == "kr" else left)
        if stream in ("vr", "vl"):
            return remote(stream, chunk, part(v_in, chunk=chunk), part(vbuf, z, chunk=chunk), right if stream == "vr" else left)
        if stream == "kf":
            slab = (z + 3) % 4
            return remote(stream, chunk, part(kbuf, slab, chunk=chunk), part(kbuf, slab, chunk=chunk), right)
        if stream == "vf":
            slab = (z + 1) % 4
            return remote(stream, chunk, part(vbuf, slab, chunk=chunk), part(vbuf, slab, chunk=chunk), left)
        if stream == "qb":
            return remote(stream, chunk, part(q_in, chunk=chunk), part(qbuf, B, chunk=chunk), near_out)
        if stream == "qc":
            return remote(stream, chunk, part(q_in, chunk=chunk), part(qbuf, C, chunk=chunk), diag_out)
        if stream == "qd0":
            return remote(stream, chunk, part(qbuf, B, chunk=chunk, lanes=first), part(qbuf, D, chunk=chunk, lanes=first), diag_in)
        if stream == "qd1":
            return remote(stream, chunk, part(qbuf, C, chunk=chunk, lanes=second), part(qbuf, D, chunk=chunk, lanes=second), near_in)
        if stream == "qe":
            return remote(stream, chunk, part(qbuf, D, chunk=chunk), part(qbuf, E, chunk=chunk), y_next)
        return remote(stream, chunk, part(qbuf, C, chunk=chunk), part(qbuf, F, chunk=chunk), y_next)

    def arrival(stream, chunk):
        if stream in ("kr", "kl", "kf"):
            slab = (z + {"kr": 3, "kl": 1, "kf": 2}[stream]) % 4
            ref = part(kbuf, slab, chunk=chunk)
        elif stream in ("vr", "vl", "vf"):
            slab = (z + {"vr": 3, "vl": 1, "vf": 2}[stream]) % 4
            ref = part(vbuf, slab, chunk=chunk)
        elif stream == "qd0":
            ref = part(qbuf, D, chunk=chunk, lanes=first)
        elif stream == "qd1":
            ref = part(qbuf, D, chunk=chunk, lanes=second)
        else:
            ref = part(qbuf, {"qb": B, "qc": C, "qe": E, "qf": F}[stream], chunk=chunk)
        return remote(stream, chunk, ref, ref, right)

    def returns(kind, chunk, target):
        at = RETURNS[kind]
        return (
            pltpu.make_async_remote_copy(
                src_ref=osend.at[at, chunk], dst_ref=orecv.at[at, chunk], send_sem=osend_sem.at[at, chunk],
                recv_sem=orecv_sem.at[at, chunk], device_id=target, device_id_type=MESH
            ),
            pltpu.make_async_remote_copy(
                src_ref=lsend.at[at, chunk], dst_ref=lrecv.at[at, chunk], send_sem=lsend_sem.at[at, chunk],
                recv_sem=lrecv_sem.at[at, chunk], device_id=target, device_id_type=MESH
            ),
        )

    back = {B: near_in, C: diag_in, D: across, E: y_prev, F: y_prev}

    def start_own(chunk):
        for stream in ("kr", "kl", "vr", "vl", "qb", "qc"):
            copy(stream, chunk).start()

    def send_back(kind, chunk, values, logs):
        at = RETURNS[kind]
        for head in range(HEADS):
            osend[at, chunk, :, head * HEAD : (head + 1) * HEAD] = values[head].astype(BF)
        stacked = jnp.concatenate(logs, axis=0)
        for block in range(3):
            lsend[at, chunk, block : block + 1, :] = stacked[block * HEAD : (block + 1) * HEAD].T[0:1, :]
        for one in returns(kind, chunk, back[kind]):
            one.start()

    def came_back(kind, chunk):
        at = RETURNS[kind]
        for one in returns(kind, chunk, back[kind]):
            one.wait_recv()
        blocks = [
            jnp.broadcast_to(lrecv[at, chunk, block : block + 1, :], (HEAD, HEAD)).T for block in range(3)
        ]
        stacked = jnp.concatenate(blocks, axis=0)
        return [
            (orecv[at, chunk, :, head * HEAD : (head + 1) * HEAD].astype(F32), stacked[head * TOK : (head + 1) * TOK])
            for head in range(HEADS)
        ]

    def kept(kind, chunk):
        at = LOCAL[kind]
        return [(okeep[at, chunk, head], lkeep[at, chunk, head]) for head in range(HEADS)]

    def attend(chunk, begin, span, sets, slabs):
        keys = pl.ds(pl.multiple_of(begin, LINE), span * LINE)
        count = FR * span * LINE
        ones = jnp.ones((count, HEAD), BF)
        results = {kind: [] for kind in sets}
        for head in range(HEADS):
            lanes = pl.ds(head * HEAD, HEAD)
            queries = qbuf[sets[0] : sets[0] + 3, :, rows_of(chunk), lanes].reshape(3 * TOK, HEAD)
            scores = [
                lax.dot_general(
                    queries, kbuf[slab, :, keys, lanes].reshape(count, HEAD), (((1,), (1,)), ((), ())),
                    preferred_element_type=F32
                )
                for slab in slabs
            ]
            top = functools.reduce(jnp.maximum, [jnp.max(one, axis=1, keepdims=True) for one in scores]) * FACTOR
            summed = None
            for slab, one in zip(slabs, scores):
                weights = jnp.exp2(one * FACTOR - top).astype(BF)
                values = jnp.concatenate([vbuf[slab, :, keys, lanes].reshape(count, HEAD), ones], axis=1)
                product = jnp.dot(weights, values, preferred_element_type=F32)
                summed = product if summed is None else summed + product
            totals = summed[:, HEAD:]
            mean = summed[:, :HEAD] / totals
            logs = top + jnp.log2(totals)
            for at, kind in enumerate(sets):
                results[kind].append((mean[at * TOK : (at + 1) * TOK], logs[at * TOK : (at + 1) * TOK]))
        for kind in sets:
            if kind in LOCAL:
                for head in range(HEADS):
                    okeep[LOCAL[kind], chunk, head], lkeep[LOCAL[kind], chunk, head] = results[kind][head]
            elif kind == B:
                send_back(kind, chunk, *zip(*results[kind]))
            else:

                @pl.when(has_prev)
                def _():
                    send_back(kind, chunk, *zip(*results[kind]))

    def attend_both(chunk, begin, span):
        attend(chunk, begin, span, (A, D, E), (0, 1, 2, 3))

        @pl.when(has_other)
        def _():
            attend(chunk, begin, span, (B, C, F), (2 - 2 * zt, 3 - 2 * zt))

    own = [
        pltpu.make_async_copy(k_in, kbuf.at[z], local_sem.at[0]),
        pltpu.make_async_copy(v_in, vbuf.at[z], local_sem.at[1]),
        pltpu.make_async_copy(q_in, qbuf.at[A], local_sem.at[2]),
    ]
    for chunk in range(3):
        start_own(chunk)
    for one in own:
        one.start()

    @pl.when(jnp.logical_not(has_prev))
    def _():
        fill = [
            pltpu.make_async_copy(q_in, qbuf.at[E], local_sem.at[3]),
            pltpu.make_async_copy(q_in, qbuf.at[F], local_sem.at[4]),
        ]
        for one in fill:
            one.start()
        for one in fill:
            one.wait()

    for one in own:
        one.wait()

    def wait_keys(chunk):
        for stream in ("kl", "vr", "kf", "vf"):
            arrival(stream, chunk).wait_recv()

    def step(turn, carry):
        now = turn - 2

        @pl.when((now >= 0) & (now + 3 < ROWS))
        def _():
            start_own(now + 3)

        @pl.when(now + 2 < ROWS)
        def _():
            chunk = now + 2
            arrival("kr", chunk).wait_recv()
            copy("kf", chunk).start()
            arrival("vl", chunk).wait_recv()
            copy("vf", chunk).start()
            arrival("qb", chunk).wait_recv()
            copy("qd0", chunk).start()
            arrival("qc", chunk).wait_recv()
            copy("qd1", chunk).start()

        @pl.when(inside(now + 1))
        def _():
            chunk = now + 1
            arrival("qd0", chunk).wait_recv()
            arrival("qd1", chunk).wait_recv()

            @pl.when(has_next)
            def _():
                copy("qe", chunk).start()

                @pl.when(has_other)
                def _():
                    copy("qf", chunk).start()

        @pl.when(inside(now))
        def _():
            @pl.when(now == 0)
            def _():
                wait_keys(0)

            @pl.when(now + 1 < ROWS)
            def _():
                wait_keys(now + 1)

            @pl.when(has_prev)
            def _():
                arrival("qe", now).wait_recv()

                @pl.when(has_other)
                def _():
                    arrival("qf", now).wait_recv()

            rim = (now == 0) | (now == ROWS - 1)

            @pl.when(rim)
            def _():
                attend_both(now, now // (ROWS - 1) * (ROWS - 2) * LINE, 2)

            @pl.when(jnp.logical_not(rim))
            def _():
                attend_both(now, (now - 1) * LINE, 3)

        @pl.when(inside(now - 1))
        def _():
            chunk = now - 1

            def pass_on(kind, extra):
                @pl.when(has_next)
                def _():
                    merged = [merge(pair) for pair in zip(kept(kind, chunk), came_back(extra, chunk))]
                    send_back(kind, chunk, *zip(*merged))

                @pl.when(jnp.logical_not(has_next))
                def _():
                    send_back(kind, chunk, *zip(*kept(kind, chunk)))

            pass_on(D, E)

            @pl.when(has_other)
            def _():
                pass_on(C, F)

        @pl.when(now - 2 >= 0)
        def _():
            chunk = now - 2

            def finish(kinds):
                parts = [kept(A, chunk)] + [came_back(kind, chunk) for kind in kinds]
                for head in range(HEADS):
                    value, _ = merge([one[head] for one in parts])
                    out[:, rows_of(chunk), head * HEAD : (head + 1) * HEAD] = value.astype(BF).reshape(FR, LINE, HEAD)

            @pl.when(sends_other)
            def _():
                finish((D, B, C))

            @pl.when(jnp.logical_not(sends_other))
            def _():
                finish((D,))

        return carry

    lax.fori_loop(0, ROWS + 4, step, 0)

    def drain(chunk, carry):
        for stream in ("kr", "kl", "vr", "vl", "kf", "vf", "qb", "qc", "qd0", "qd1"):
            copy(stream, chunk).wait_send()

        def sent(kind):
            for one in returns(kind, chunk, back[kind]):
                one.wait_send()

        sent(D)

        @pl.when(has_other)
        def _():
            sent(B)
            sent(C)

            @pl.when(has_prev)
            def _():
                sent(F)

            @pl.when(has_next)
            def _():
                copy("qf", chunk).wait_send()

        @pl.when(has_prev)
        def _():
            sent(E)

        @pl.when(has_next)
        def _():
            copy("qe", chunk).wait_send()

        return carry

    lax.fori_loop(0, ROWS, drain, 0)


def per_device(queries, key_field, value_field):
    shape = queries.shape
    flat = (FR, ROWS * LINE, HEADS * HEAD)
    args = [one.reshape(flat) for one in (queries, key_field, value_field)]
    anywhere = pl.BlockSpec(memory_space=pl.ANY)
    result = pl.pallas_call(
        kernel,
        out_shape=jax.ShapeDtypeStruct(flat, BF),
        in_specs=[anywhere] * 3,
        out_specs=pl.BlockSpec(memory_space=pltpu.VMEM),
        scratch_shapes=[
            pltpu.VMEM((4, *flat), BF),
            pltpu.VMEM((4, *flat), BF),
            pltpu.VMEM((6, *flat), BF),
            pltpu.VMEM((3, ROWS, HEADS, TOK, HEAD), F32),
            pltpu.VMEM((3, ROWS, HEADS, TOK, HEAD), F32),
            pltpu.VMEM((5, ROWS, TOK, HEADS * HEAD), BF),
            pltpu.VMEM((5, ROWS, 8, HEAD), F32),
            pltpu.VMEM((5, ROWS, TOK, HEADS * HEAD), BF),
            pltpu.VMEM((5, ROWS, 8, HEAD), F32),
            pltpu.SemaphoreType.DMA((5,)),
            pltpu.SemaphoreType.DMA((len(STREAMS), ROWS)),
            pltpu.SemaphoreType.DMA((len(STREAMS), ROWS)),
            pltpu.SemaphoreType.DMA((5, ROWS)),
            pltpu.SemaphoreType.DMA((5, ROWS)),
            pltpu.SemaphoreType.DMA((5, ROWS)),
            pltpu.SemaphoreType.DMA((5, ROWS)),
        ],
        compiler_params=pltpu.CompilerParams(
            collective_id=0, has_side_effects=True, vmem_limit_bytes=60 * 2**20
        ),
        name="tile_attention",
    )(*args)
    return result.reshape(shape)


def solution(mesh):
    spec = P(("ta", "ha"), None, "wa", None)
    return jax.shard_map(per_device, mesh=mesh, in_specs=(spec,) * 3, out_specs=spec, check_vma=False)
```

```python
import functools

import jax
import jax.numpy as jnp
from jax import lax
from jax.experimental import pallas as pl
from jax.experimental.pallas import tpu as pltpu
from jax.sharding import PartitionSpec as P

HEAD = 128
HEADS = 2
ROWS = 8
FR = 3
LINE = 64
HALF = LINE // 2
TOK = FR * LINE
FACTOR = HEAD**-0.5 * 1.4426950408889634
MESH = pl.DeviceIdType.MESH
BF = jnp.bfloat16
F32 = jnp.float32

A, D, E, B, C, F = range(6)
BLOCK = 768
STREAMS = ("kr", "kl", "vr", "vl", "kf", "vf", "qb", "qc", "qd0", "qd1", "qe", "qf")
RETURNS = {B: 0, C: 1, D: 2, E: 3, F: 4}
LOCAL = {A: 0, D: 1, C: 2}


def rows_of(chunk):
    return pl.ds(pl.multiple_of(chunk * LINE, LINE), LINE)


def merge(parts):
    top = functools.reduce(jnp.maximum, [log for _, log in parts])
    shares = [jnp.exp2(log - top) for _, log in parts]
    total = functools.reduce(jnp.add, shares)
    value = functools.reduce(jnp.add, [share * out for share, (out, _) in zip(shares, parts)])
    return value / total, top + jnp.log2(total)


def kernel(
    q_in, k_in, v_in, out, kbuf, vbuf, qbuf, okeep, lkeep, osend, lsend, orecv, lrecv, local_sem, send_sem, recv_sem,
    osend_sem, orecv_sem, lsend_sem, lrecv_sem, done, out_sem
):
    core = lax.axis_index("ta")
    ha = lax.axis_index("ha")
    wa = lax.axis_index("wa")
    z, x_lo, y, x_hi = ha % 4, ha // 4, wa // 2, wa % 2
    zt = z // 2

    def device(lo, hi, yy, zz, cc):
        return {"ta": cc, "ha": lo * 4 + zz, "wa": yy * 2 + hi}

    swap = 1 - (x_lo + zt) % 2
    out_core = (core + swap) % 2
    in_core = (core + 1 - swap) % 2
    has_other = (swap == 1) | (core == zt)
    sends_other = (swap == 0) | (core != zt)
    right = device(x_lo, x_hi, y, (z + 1) % 4, core)
    left = device(x_lo, x_hi, y, (z + 3) % 4, core)
    step_y = 1 - 2 * x_hi
    y_next = device(x_lo, x_hi, (y + step_y + 4) % 4, z, core)
    y_prev = device(x_lo, x_hi, (y - step_y + 4) % 4, z, core)
    y_first = 3 * x_hi
    has_prev = y != y_first
    has_next = y != 3 - y_first
    near_out = device(1 - x_lo, x_hi, y, z, out_core)
    near_in = device(1 - x_lo, x_hi, y, z, in_core)
    diag_out = device(1 - x_lo, 1 - x_hi, y, z, out_core)
    diag_in = device(1 - x_lo, 1 - x_hi, y, z, in_core)
    across = device(x_lo, 1 - x_hi, y, z, core)

    barrier = pltpu.get_barrier_semaphore()
    peers = (right, left, y_next, y_prev, near_out, near_in, diag_out, diag_in, across)
    for peer in peers:
        pl.semaphore_signal(barrier, inc=1, device_id=peer, device_id_type=MESH)
    pl.semaphore_wait(barrier, len(peers))

    def remote(stream, chunk, src, dst, target):
        at = STREAMS.index(stream)
        return pltpu.make_async_remote_copy(
            src_ref=src, dst_ref=dst, send_sem=send_sem.at[at, chunk], recv_sem=recv_sem.at[at, chunk],
            device_id=target, device_id_type=MESH
        )

    def part(ref, *lead, chunk, half=None):
        rows = rows_of(chunk) if half is None else pl.ds(pl.multiple_of(chunk * LINE + half * HALF, HALF), HALF)
        return ref.at[(*lead, slice(None), rows, slice(None))]

    def copy(stream, chunk):
        if stream in ("kr", "kl"):
            return remote(stream, chunk, part(k_in, chunk=chunk), part(kbuf, z, chunk=chunk), right if stream == "kr" else left)
        if stream in ("vr", "vl"):
            return remote(stream, chunk, part(v_in, chunk=chunk), part(vbuf, z, chunk=chunk), right if stream == "vr" else left)
        if stream == "kf":
            slab = (z + 3) % 4
            return remote(stream, chunk, part(kbuf, slab, chunk=chunk), part(kbuf, slab, chunk=chunk), right)
        if stream == "vf":
            slab = (z + 1) % 4
            return remote(stream, chunk, part(vbuf, slab, chunk=chunk), part(vbuf, slab, chunk=chunk), left)
        if stream == "qb":
            return remote(stream, chunk, part(q_in, chunk=chunk), part(qbuf, B, chunk=chunk), near_out)
        if stream == "qc":
            return remote(stream, chunk, part(q_in, chunk=chunk), part(qbuf, C, chunk=chunk), diag_out)
        if stream == "qd0":
            return remote(stream, chunk, part(qbuf, B, chunk=chunk, half=0), part(qbuf, D, chunk=chunk, half=0), diag_in)
        if stream == "qd1":
            return remote(stream, chunk, part(qbuf, C, chunk=chunk, half=1), part(qbuf, D, chunk=chunk, half=1), near_in)
        if stream == "qe":
            return remote(stream, chunk, part(qbuf, D, chunk=chunk), part(qbuf, E, chunk=chunk), y_next)
        return remote(stream, chunk, part(qbuf, C, chunk=chunk), part(qbuf, F, chunk=chunk), y_next)

    def arrival(stream, chunk):
        if stream in ("kr", "kl", "kf"):
            slab = (z + {"kr": 3, "kl": 1, "kf": 2}[stream]) % 4
            ref = part(kbuf, slab, chunk=chunk)
        elif stream in ("vr", "vl", "vf"):
            slab = (z + {"vr": 3, "vl": 1, "vf": 2}[stream]) % 4
            ref = part(vbuf, slab, chunk=chunk)
        elif stream == "qd0":
            ref = part(qbuf, D, chunk=chunk, half=0)
        elif stream == "qd1":
            ref = part(qbuf, D, chunk=chunk, half=1)
        else:
            ref = part(qbuf, {"qb": B, "qc": C, "qe": E, "qf": F}[stream], chunk=chunk)
        return remote(stream, chunk, ref, ref, right)

    def returns(kind, chunk, target):
        at = RETURNS[kind]
        return (
            pltpu.make_async_remote_copy(
                src_ref=osend.at[at, chunk], dst_ref=orecv.at[at, chunk], send_sem=osend_sem.at[at, chunk],
                recv_sem=orecv_sem.at[at, chunk], device_id=target, device_id_type=MESH
            ),
            pltpu.make_async_remote_copy(
                src_ref=lsend.at[at, chunk], dst_ref=lrecv.at[at, chunk], send_sem=lsend_sem.at[at, chunk],
                recv_sem=lrecv_sem.at[at, chunk], device_id=target, device_id_type=MESH
            ),
        )

    back = {B: near_in, C: diag_in, D: across, E: y_prev, F: y_prev}

    def start_own(chunk):
        for stream in ("kr", "kl", "vr", "vl", "qb", "qc"):
            copy(stream, chunk).start()

    lane = lax.broadcasted_iota(jnp.int32, (HEAD, HEAD), 1)
    eye = lane == lax.broadcasted_iota(jnp.int32, (HEAD, HEAD), 0)

    def put_back(kind, slot, head, value, log):
        at = RETURNS[kind]
        osend[at, slot, :, head * HEAD : (head + 1) * HEAD] = value.astype(BF)
        for half, (begin, size) in enumerate(((0, HEAD), (HEAD, TOK - HEAD))):
            picked = jnp.where(eye[:size], log[begin : begin + size], 0.0)
            row = 2 * head + half
            lsend[at, slot, row : row + 1, :] = jnp.sum(picked, axis=0, keepdims=True)

    def came_back(kind, slot, head):
        at = RETURNS[kind]
        logs = []
        for half, size in enumerate((HEAD, TOK - HEAD)):
            row = 2 * head + half
            spread = jnp.broadcast_to(lrecv[at, slot, row : row + 1, :], (size, HEAD))
            logs.append(jnp.sum(jnp.where(eye[:size], spread, 0.0), axis=1, keepdims=True))
        log = jnp.broadcast_to(jnp.concatenate(logs, axis=0), (TOK, HEAD))
        return orecv[at, slot, :, head * HEAD : (head + 1) * HEAD].astype(F32), log

    def kept(kind, slot, head):
        return okeep[LOCAL[kind], slot, head], lkeep[LOCAL[kind], slot, head]

    def pass_on(slot, head):
        for kind, extra in ((D, E), (C, F)):
            put_back(kind, slot, head, *merge([kept(kind, slot, head), came_back(extra, slot, head)]))

    def finish(slot, head):
        parts = [kept(A, slot, head)] + [came_back(kind, slot, head) for kind in (D, B, C)]
        value, _ = merge(parts)
        done[slot, :, :, head * HEAD : (head + 1) * HEAD] = value.astype(BF).reshape(FR, LINE, HEAD)

    def attend(chunk, begin, span, extras):
        keys = pl.ds(pl.multiple_of(begin, LINE), span * LINE)
        groups = (((A, D, E), (0, 1, 2, 3)), ((B, C, F), (2 - 2 * zt, 3 - 2 * zt)))
        jobs = [(sets, slabs, head) for sets, slabs in groups for head in range(HEADS)]

        def pieces(ref, slabs, lanes):
            whole = jnp.concatenate(
                [ref[slab, :, keys, lanes].reshape(FR * span * LINE, HEAD) for slab in slabs], axis=0
            )
            return [whole[at : at + BLOCK] for at in range(0, whole.shape[0], BLOCK)]

        def products(job):
            sets, slabs, head = job
            lanes = pl.ds(head * HEAD, HEAD)
            queries = qbuf[sets[0] : sets[0] + 3, :, rows_of(chunk), lanes].reshape(3 * TOK, HEAD)
            return [
                lax.dot_general(queries, piece, (((1,), (1,)), ((), ())), preferred_element_type=F32)
                for piece in pieces(kbuf, slabs, lanes)
            ]

        scores = products(jobs[0])
        for number, (sets, slabs, head) in enumerate(jobs):
            later = products(jobs[number + 1]) if number + 1 < len(jobs) else None
            columns = [one[:, at : at + HEAD] for one in scores for at in range(0, one.shape[1], HEAD)]
            top = jnp.max(functools.reduce(jnp.maximum, columns), axis=1, keepdims=True) * FACTOR
            summed = None
            for one, piece in zip(scores, pieces(vbuf, slabs, pl.ds(head * HEAD, HEAD))):
                weights = jnp.exp2(one * FACTOR - top).astype(BF)
                product = jnp.dot(
                    weights, jnp.concatenate([piece, jnp.ones_like(piece)], axis=1), preferred_element_type=F32
                )
                summed = product if summed is None else summed + product
            totals = summed[:, HEAD:]
            mean = summed[:, :HEAD] / totals
            logs = top + jnp.log2(totals)
            for at, kind in enumerate(sets):
                value, log = mean[at * TOK : (at + 1) * TOK], logs[at * TOK : (at + 1) * TOK]
                if kind in LOCAL:
                    okeep[LOCAL[kind], chunk, head], lkeep[LOCAL[kind], chunk, head] = value, log
                else:
                    put_back(kind, chunk, head, value, log)
            scores = later
            for extra in extras[number]:
                extra()

    def start_back(kind, chunk):
        for one in returns(kind, chunk, back[kind]):
            one.start()

    def wait_back(kind, chunk):
        for one in returns(kind, chunk, back[kind]):
            one.wait_recv()

    own = [
        pltpu.make_async_copy(k_in, kbuf.at[z], local_sem.at[0]),
        pltpu.make_async_copy(v_in, vbuf.at[z], local_sem.at[1]),
        pltpu.make_async_copy(q_in, qbuf.at[A], local_sem.at[2]),
    ]
    for chunk in range(2):
        start_own(chunk)
    for one in own:
        one.start()

    @pl.when(jnp.logical_not(has_prev))
    def _():
        fill = pltpu.make_async_copy(q_in, qbuf.at[E], local_sem.at[3])
        fill.start()
        fill.wait()

    @pl.when(jnp.logical_not(has_prev & has_other))
    def _():
        fill = pltpu.make_async_copy(q_in, qbuf.at[F], local_sem.at[4])
        fill.start()
        fill.wait()

    def absent(kind):
        def blank(slot, carry):
            orecv[RETURNS[kind], slot] = jnp.zeros((TOK, HEADS * HEAD), BF)
            lrecv[RETURNS[kind], slot] = jnp.full((8, HEAD), -1e30, F32)
            return carry

        lax.fori_loop(0, ROWS, blank, 0)

    @pl.when(jnp.logical_not(has_next))
    def _():
        absent(E)

    @pl.when(jnp.logical_not(has_next & has_other))
    def _():
        absent(F)

    @pl.when(jnp.logical_not(sends_other))
    def _():
        absent(B)
        absent(C)

    for one in own:
        one.wait()

    def forward(chunk):
        arrival("kr", chunk).wait_recv()
        copy("kf", chunk).start()
        arrival("vl", chunk).wait_recv()
        copy("vf", chunk).start()
        arrival("qb", chunk).wait_recv()
        copy("qd0", chunk).start()
        arrival("qc", chunk).wait_recv()
        copy("qd1", chunk).start()

    def forward_across(chunk):
        arrival("qd0", chunk).wait_recv()
        arrival("qd1", chunk).wait_recv()

        @pl.when(has_next)
        def _():
            copy("qe", chunk).start()

            @pl.when(has_other)
            def _():
                copy("qf", chunk).start()

    def wait_keys(chunk):
        for stream in ("kl", "vr", "kf", "vf"):
            arrival(stream, chunk).wait_recv()

    def wait_queries(chunk):
        @pl.when(has_prev)
        def _():
            arrival("qe", chunk).wait_recv()

            @pl.when(has_other)
            def _():
                arrival("qf", chunk).wait_recv()

    def wait_sides(chunk):
        @pl.when(has_next)
        def _():
            wait_back(E, chunk)

            @pl.when(has_other)
            def _():
                wait_back(F, chunk)

    def wait_home(chunk):
        wait_back(D, chunk)

        @pl.when(sends_other)
        def _():
            wait_back(B, chunk)
            wait_back(C, chunk)

    def start_sides(chunk):
        @pl.when(has_prev)
        def _():
            start_back(E, chunk)

            @pl.when(has_other)
            def _():
                start_back(F, chunk)

        @pl.when(has_other)
        def _():
            start_back(B, chunk)

    def start_home(chunk):
        start_back(D, chunk)

        @pl.when(has_other)
        def _():
            start_back(C, chunk)

    def stored(chunk):
        return pltpu.make_async_copy(done.at[chunk], out.at[:, rows_of(chunk), :], out_sem.at[chunk])

    def spare(chunk):
        there = (chunk + ROWS) // ROWS
        return there * chunk + (1 - there) * ROWS

    def merging(passed, finished):
        work = [
            functools.partial(one, slot, head)
            for one, slot in ((pass_on, passed), (finish, finished))
            for head in range(HEADS)
        ]
        return [[one] for one in work]

    forward(0)
    start_own(2)
    forward(1)
    start_own(3)
    forward_across(0)
    forward(2)
    start_own(4)
    forward_across(1)
    wait_keys(0)
    wait_keys(1)
    wait_queries(0)
    attend(0, 0, 2, [[]] * 4)
    start_sides(0)

    def step(now, carry):
        @pl.when(now + 2 < ROWS)
        def _():
            forward(now + 2)

        @pl.when(now + 4 < ROWS)
        def _():
            start_own(now + 4)

        forward_across(now + 1)
        wait_keys(now + 1)
        wait_queries(now)

        @pl.when(now >= 2)
        def _():
            wait_sides(now - 2)

        @pl.when(now >= 4)
        def _():
            wait_home(now - 4)

        attend(now, (now - 1) * LINE, 3, merging(spare(now - 2), spare(now - 4)))
        start_sides(now)

        @pl.when(now >= 2)
        def _():
            start_home(now - 2)

        @pl.when(now >= 4)
        def _():
            stored(now - 4).start()

        return carry

    lax.fori_loop(1, ROWS - 1, step, 0)

    last = ROWS - 1
    wait_queries(last)
    wait_sides(last - 2)
    wait_home(last - 4)
    attend(last, (last - 1) * LINE, 2, merging(last - 2, last - 4))
    start_sides(last)
    start_home(last - 2)
    stored(last - 4).start()

    def pass_last(chunk):
        wait_sides(chunk)
        for head in range(HEADS):
            pass_on(chunk, head)
        start_home(chunk)

    def finish_last(chunk):
        wait_home(chunk)
        for head in range(HEADS):
            finish(chunk, head)
        stored(chunk).start()

    pass_last(last - 1)
    finish_last(last - 3)
    finish_last(last - 2)
    pass_last(last)
    finish_last(last - 1)
    finish_last(last)

    def drain(chunk, carry):
        for stream in ("kr", "kl", "vr", "vl", "kf", "vf", "qb", "qc", "qd0", "qd1"):
            copy(stream, chunk).wait_send()
        stored(chunk).wait()

        def sent(kind):
            for one in returns(kind, chunk, back[kind]):
                one.wait_send()

        sent(D)

        @pl.when(has_other)
        def _():
            sent(B)
            sent(C)

            @pl.when(has_prev)
            def _():
                sent(F)

            @pl.when(has_next)
            def _():
                copy("qf", chunk).wait_send()

        @pl.when(has_prev)
        def _():
            sent(E)

        @pl.when(has_next)
        def _():
            copy("qe", chunk).wait_send()

        return carry

    lax.fori_loop(0, ROWS, drain, 0)


def per_device(queries, key_field, value_field):
    shape = queries.shape
    flat = (FR, ROWS * LINE, HEADS * HEAD)
    args = [one.reshape(flat) for one in (queries, key_field, value_field)]
    anywhere = pl.BlockSpec(memory_space=pl.ANY)
    result = pl.pallas_call(
        kernel,
        out_shape=jax.ShapeDtypeStruct(flat, BF),
        in_specs=[anywhere] * 3,
        out_specs=anywhere,
        scratch_shapes=[
            pltpu.VMEM((4, *flat), BF),
            pltpu.VMEM((4, *flat), BF),
            pltpu.VMEM((6, *flat), BF),
            pltpu.VMEM((3, ROWS + 1, HEADS, TOK, HEAD), F32),
            pltpu.VMEM((3, ROWS + 1, HEADS, TOK, HEAD), F32),
            pltpu.VMEM((5, ROWS + 1, TOK, HEADS * HEAD), BF),
            pltpu.VMEM((5, ROWS + 1, 8, HEAD), F32),
            pltpu.VMEM((5, ROWS + 1, TOK, HEADS * HEAD), BF),
            pltpu.VMEM((5, ROWS + 1, 8, HEAD), F32),
            pltpu.SemaphoreType.DMA((5,)),
            pltpu.SemaphoreType.DMA((len(STREAMS), ROWS)),
            pltpu.SemaphoreType.DMA((len(STREAMS), ROWS)),
            pltpu.SemaphoreType.DMA((5, ROWS)),
            pltpu.SemaphoreType.DMA((5, ROWS)),
            pltpu.SemaphoreType.DMA((5, ROWS)),
            pltpu.SemaphoreType.DMA((5, ROWS)),
            pltpu.VMEM((ROWS + 1, FR, LINE, HEADS * HEAD), BF),
            pltpu.SemaphoreType.DMA((ROWS,)),
        ],
        compiler_params=pltpu.CompilerParams(
            collective_id=0, has_side_effects=True, vmem_limit_bytes=60 * 2**20
        ),
        name="tile_attention",
    )(*args)
    return result.reshape(shape)


def solution(mesh):
    spec = P(("ta", "ha"), None, "wa", None)
    return jax.shard_map(per_device, mesh=mesh, in_specs=(spec,) * 3, out_specs=spec, check_vma=False)
```

```python
import functools

import jax
import jax.numpy as jnp
from jax import lax
from jax.experimental import pallas as pl
from jax.experimental.pallas import tpu as pltpu
from jax.sharding import PartitionSpec as P

HEAD = 128
HEADS = 2
ROWS = 8
FR = 3
LINE = 64
HALF = LINE // 2
TOK = FR * LINE
FACTOR = HEAD**-0.5 * 1.4426950408889634
MESH = pl.DeviceIdType.MESH
BF = jnp.bfloat16
F32 = jnp.float32

A, D, E, B, C, F = range(6)
BLOCK = 768
STREAMS = ("kr", "kl", "vr", "vl", "kf", "vf", "qb", "qc", "qd0", "qd1", "qe", "qf")
RETURNS = {B: 0, C: 1, D: 2, E: 3, F: 4}
LOCAL = {A: 0, D: 1, C: 2}


def rows_of(chunk):
    return pl.ds(pl.multiple_of(chunk * LINE, LINE), LINE)


def merge(parts):
    top = functools.reduce(jnp.maximum, [log for _, log in parts])
    shares = [jnp.exp2(log - top) for _, log in parts]
    total = functools.reduce(jnp.add, shares)
    value = functools.reduce(jnp.add, [share * out for share, (out, _) in zip(shares, parts)])
    return value / total, top + jnp.log2(total)


def kernel(
    q_in, k_in, v_in, out, kbuf, vbuf, qbuf, okeep, lkeep, osend, lsend, orecv, lrecv, local_sem, send_sem, recv_sem,
    osend_sem, orecv_sem, lsend_sem, lrecv_sem, done, out_sem
):
    core = lax.axis_index("ta")
    ha = lax.axis_index("ha")
    wa = lax.axis_index("wa")
    z, x_lo, y, x_hi = ha % 4, ha // 4, wa // 2, wa % 2
    zt = z // 2

    def device(lo, hi, yy, zz, cc):
        return {"ta": cc, "ha": lo * 4 + zz, "wa": yy * 2 + hi}

    swap = 1 - (x_lo + zt) % 2
    out_core = (core + swap) % 2
    in_core = (core + 1 - swap) % 2
    has_other = (swap == 1) | (core == zt)
    sends_other = (swap == 0) | (core != zt)
    right = device(x_lo, x_hi, y, (z + 1) % 4, core)
    left = device(x_lo, x_hi, y, (z + 3) % 4, core)
    step_y = 1 - 2 * x_hi
    y_next = device(x_lo, x_hi, (y + step_y + 4) % 4, z, core)
    y_prev = device(x_lo, x_hi, (y - step_y + 4) % 4, z, core)
    y_first = 3 * x_hi
    has_prev = y != y_first
    has_next = y != 3 - y_first
    near_out = device(1 - x_lo, x_hi, y, z, out_core)
    near_in = device(1 - x_lo, x_hi, y, z, in_core)
    diag_out = device(1 - x_lo, 1 - x_hi, y, z, out_core)
    diag_in = device(1 - x_lo, 1 - x_hi, y, z, in_core)
    across = device(x_lo, 1 - x_hi, y, z, core)

    barrier = pltpu.get_barrier_semaphore()
    peers = (right, left, y_next, y_prev, near_out, near_in, diag_out, diag_in, across)
    for peer in peers:
        pl.semaphore_signal(barrier, inc=1, device_id=peer, device_id_type=MESH)
    pl.semaphore_wait(barrier, len(peers))

    def remote(stream, chunk, src, dst, target):
        at = STREAMS.index(stream)
        return pltpu.make_async_remote_copy(
            src_ref=src, dst_ref=dst, send_sem=send_sem.at[at, chunk], recv_sem=recv_sem.at[at, chunk],
            device_id=target, device_id_type=MESH
        )

    def part(ref, *lead, chunk, half=None):
        rows = rows_of(chunk) if half is None else pl.ds(pl.multiple_of(chunk * LINE + half * HALF, HALF), HALF)
        return ref.at[(*lead, slice(None), rows, slice(None))]

    def copy(stream, chunk, half=None):
        if stream in ("kr", "kl"):
            return remote(stream, chunk, part(k_in, chunk=chunk), part(kbuf, z, chunk=chunk), right if stream == "kr" else left)
        if stream in ("vr", "vl"):
            return remote(stream, chunk, part(v_in, chunk=chunk), part(vbuf, z, chunk=chunk), right if stream == "vr" else left)
        if stream == "kf":
            slab = (z + 3) % 4
            return remote(stream, chunk, part(kbuf, slab, chunk=chunk), part(kbuf, slab, chunk=chunk), right)
        if stream == "vf":
            slab = (z + 1) % 4
            return remote(stream, chunk, part(vbuf, slab, chunk=chunk), part(vbuf, slab, chunk=chunk), left)
        if stream == "qb":
            return remote(stream, chunk, part(q_in, chunk=chunk, half=half), part(qbuf, B, chunk=chunk, half=half), near_out)
        if stream == "qc":
            return remote(stream, chunk, part(q_in, chunk=chunk, half=half), part(qbuf, C, chunk=chunk, half=half), diag_out)
        if stream == "qd0":
            return remote(stream, chunk, part(qbuf, B, chunk=chunk, half=0), part(qbuf, D, chunk=chunk, half=0), diag_in)
        if stream == "qd1":
            return remote(stream, chunk, part(qbuf, C, chunk=chunk, half=1), part(qbuf, D, chunk=chunk, half=1), near_in)
        if stream == "qe":
            return remote(stream, chunk, part(qbuf, D, chunk=chunk), part(qbuf, E, chunk=chunk), y_next)
        return remote(stream, chunk, part(qbuf, C, chunk=chunk), part(qbuf, F, chunk=chunk), y_next)

    def arrival(stream, chunk, half=None):
        if stream in ("kr", "kl", "kf"):
            slab = (z + {"kr": 3, "kl": 1, "kf": 2}[stream]) % 4
            ref = part(kbuf, slab, chunk=chunk)
        elif stream in ("vr", "vl", "vf"):
            slab = (z + {"vr": 3, "vl": 1, "vf": 2}[stream]) % 4
            ref = part(vbuf, slab, chunk=chunk)
        elif stream == "qd0":
            ref = part(qbuf, D, chunk=chunk, half=0)
        elif stream == "qd1":
            ref = part(qbuf, D, chunk=chunk, half=1)
        else:
            ref = part(qbuf, {"qb": B, "qc": C, "qe": E, "qf": F}[stream], chunk=chunk, half=half)
        return remote(stream, chunk, ref, ref, right)

    def returns(kind, chunk, target):
        at = RETURNS[kind]
        return (
            pltpu.make_async_remote_copy(
                src_ref=osend.at[at, chunk], dst_ref=orecv.at[at, chunk], send_sem=osend_sem.at[at, chunk],
                recv_sem=orecv_sem.at[at, chunk], device_id=target, device_id_type=MESH
            ),
            pltpu.make_async_remote_copy(
                src_ref=lsend.at[at, chunk], dst_ref=lrecv.at[at, chunk], send_sem=lsend_sem.at[at, chunk],
                recv_sem=lrecv_sem.at[at, chunk], device_id=target, device_id_type=MESH
            ),
        )

    back = {B: near_in, C: diag_in, D: across, E: y_prev, F: y_prev}

    only = {B: 0, C: 1}

    def each_half(whole, *actions):
        @pl.when(whole)
        def _():
            for action in actions:
                action({B: None, C: None})

        @pl.when(jnp.logical_not(whole))
        def _():
            for action in actions:
                action(only)

    lane = lax.broadcasted_iota(jnp.int32, (HEAD, HEAD), 1)
    eye = lane == lax.broadcasted_iota(jnp.int32, (HEAD, HEAD), 0)

    def put_back(kind, slot, head, value, log):
        at = RETURNS[kind]
        osend[at, slot, :, head * HEAD : (head + 1) * HEAD] = value.astype(BF)
        for half, (begin, size) in enumerate(((0, HEAD), (HEAD, TOK - HEAD))):
            picked = jnp.where(eye[:size], log[begin : begin + size], 0.0)
            row = 2 * head + half
            lsend[at, slot, row : row + 1, :] = jnp.sum(picked, axis=0, keepdims=True)

    def came_back(kind, slot, head):
        at = RETURNS[kind]
        logs = []
        for half, size in enumerate((HEAD, TOK - HEAD)):
            row = 2 * head + half
            spread = jnp.broadcast_to(lrecv[at, slot, row : row + 1, :], (size, HEAD))
            logs.append(jnp.sum(jnp.where(eye[:size], spread, 0.0), axis=1, keepdims=True))
        log = jnp.broadcast_to(jnp.concatenate(logs, axis=0), (TOK, HEAD))
        return orecv[at, slot, :, head * HEAD : (head + 1) * HEAD].astype(F32), log

    def kept(kind, slot, head):
        return okeep[LOCAL[kind], slot, head], lkeep[LOCAL[kind], slot, head]

    def pass_on(slot, head):
        for kind, extra in ((D, E), (C, F)):
            put_back(kind, slot, head, *merge([kept(kind, slot, head), came_back(extra, slot, head)]))

    def finish(slot, head):
        parts = [kept(A, slot, head)] + [came_back(kind, slot, head) for kind in (D, B, C)]
        value, _ = merge(parts)
        done[slot, :, :, head * HEAD : (head + 1) * HEAD] = value.astype(BF).reshape(FR, LINE, HEAD)

    def attend(chunk, begin, span, extras):
        keys = pl.ds(pl.multiple_of(begin, LINE), span * LINE)
        groups = (((A, D, E), (0, 1, 2, 3)), ((B, C, F), (2 - 2 * zt, 3 - 2 * zt)))
        jobs = [(sets, slabs, head) for sets, slabs in groups for head in range(HEADS)]

        def pieces(ref, slabs, lanes):
            whole = jnp.concatenate(
                [ref[slab, :, keys, lanes].reshape(FR * span * LINE, HEAD) for slab in slabs], axis=0
            )
            return [whole[at : at + BLOCK] for at in range(0, whole.shape[0], BLOCK)]

        def products(job):
            sets, slabs, head = job
            lanes = pl.ds(head * HEAD, HEAD)
            queries = qbuf[sets[0] : sets[0] + 3, :, rows_of(chunk), lanes].reshape(3 * TOK, HEAD)
            return [
                lax.dot_general(queries, piece, (((1,), (1,)), ((), ())), preferred_element_type=F32)
                for piece in pieces(kbuf, slabs, lanes)
            ]

        scores = products(jobs[0])
        for number, (sets, slabs, head) in enumerate(jobs):
            later = products(jobs[number + 1]) if number + 1 < len(jobs) else None
            columns = [one[:, at : at + HEAD] for one in scores for at in range(0, one.shape[1], HEAD)]
            top = jnp.max(functools.reduce(jnp.maximum, columns), axis=1, keepdims=True) * FACTOR
            summed = None
            for one, piece in zip(scores, pieces(vbuf, slabs, pl.ds(head * HEAD, HEAD))):
                weights = jnp.exp2(one * FACTOR - top).astype(BF)
                product = jnp.dot(
                    weights, jnp.concatenate([piece, jnp.ones_like(piece)], axis=1), preferred_element_type=F32
                )
                summed = product if summed is None else summed + product
            totals = summed[:, HEAD:]
            mean = summed[:, :HEAD] / totals
            logs = top + jnp.log2(totals)
            for at, kind in enumerate(sets):
                value, log = mean[at * TOK : (at + 1) * TOK], logs[at * TOK : (at + 1) * TOK]
                if kind in LOCAL:
                    okeep[LOCAL[kind], chunk, head], lkeep[LOCAL[kind], chunk, head] = value, log
                else:
                    put_back(kind, chunk, head, value, log)
            scores = later
            for extra in extras[number]:
                extra()

    def start_back(kind, chunk):
        for one in returns(kind, chunk, back[kind]):
            one.start()

    def wait_back(kind, chunk):
        for one in returns(kind, chunk, back[kind]):
            one.wait_recv()

    own = [
        pltpu.make_async_copy(k_in, kbuf.at[z], local_sem.at[0]),
        pltpu.make_async_copy(v_in, vbuf.at[z], local_sem.at[1]),
        pltpu.make_async_copy(q_in, qbuf.at[A], local_sem.at[2]),
    ]
    def start_local():
        for one in own:
            one.start()
        fill_absent()

    def wait_local():
        for one in own:
            one.wait()

    def fill_absent():
        @pl.when(jnp.logical_not(has_prev))
        def _():
            fill = pltpu.make_async_copy(q_in, qbuf.at[E], local_sem.at[3])
            fill.start()
            fill.wait()

        @pl.when(jnp.logical_not(has_prev & has_other))
        def _():
            fill = pltpu.make_async_copy(q_in, qbuf.at[F], local_sem.at[4])
            fill.start()
            fill.wait()

        def absent(kind):
            def blank(slot, carry):
                orecv[RETURNS[kind], slot] = jnp.zeros((TOK, HEADS * HEAD), BF)
                lrecv[RETURNS[kind], slot] = jnp.full((8, HEAD), -1e30, F32)
                return carry

            lax.fori_loop(0, ROWS, blank, 0)

        @pl.when(jnp.logical_not(has_next))
        def _():
            absent(E)

        @pl.when(jnp.logical_not(has_next & has_other))
        def _():
            absent(F)

        @pl.when(jnp.logical_not(sends_other))
        def _():
            absent(B)
            absent(C)

    def start_kept(chunk):
        copy("kl", chunk).start()
        copy("vr", chunk).start()

    def start_passed(chunk):
        copy("kr", chunk).start()
        copy("vl", chunk).start()

    def pass_keys(chunk):
        arrival("kr", chunk).wait_recv()
        copy("kf", chunk).start()
        arrival("vl", chunk).wait_recv()
        copy("vf", chunk).start()

    def start_queries(chunk):
        each_half(
            sends_other,
            lambda half: copy("qb", chunk, half[B]).start(),
            lambda half: copy("qc", chunk, half[C]).start(),
        )

    def pass_queries(chunk):
        each_half(
            has_other,
            lambda half: arrival("qb", chunk, half[B]).wait_recv(),
            lambda half: arrival("qc", chunk, half[C]).wait_recv(),
        )
        copy("qd0", chunk).start()
        copy("qd1", chunk).start()

    def forward_across(chunk):
        arrival("qd0", chunk).wait_recv()
        arrival("qd1", chunk).wait_recv()

        @pl.when(has_next)
        def _():
            copy("qe", chunk).start()

            @pl.when(has_other)
            def _():
                copy("qf", chunk).start()

    def wait_keys(chunk):
        for stream in ("kl", "vr", "kf", "vf"):
            arrival(stream, chunk).wait_recv()

    def wait_queries(chunk):
        @pl.when(has_prev)
        def _():
            arrival("qe", chunk).wait_recv()

            @pl.when(has_other)
            def _():
                arrival("qf", chunk).wait_recv()

    def wait_sides(chunk):
        @pl.when(has_next)
        def _():
            wait_back(E, chunk)

            @pl.when(has_other)
            def _():
                wait_back(F, chunk)

    def wait_home(chunk):
        wait_back(D, chunk)

        @pl.when(sends_other)
        def _():
            wait_back(B, chunk)
            wait_back(C, chunk)

    def start_sides(chunk):
        @pl.when(has_prev)
        def _():
            start_back(E, chunk)

            @pl.when(has_other)
            def _():
                start_back(F, chunk)

        @pl.when(has_other)
        def _():
            start_back(B, chunk)

    def start_home(chunk):
        start_back(D, chunk)

        @pl.when(has_other)
        def _():
            start_back(C, chunk)

    def stored(chunk):
        return pltpu.make_async_copy(done.at[chunk], out.at[:, rows_of(chunk), :], out_sem.at[chunk])

    def spare(chunk):
        there = (chunk + ROWS) // ROWS
        return there * chunk + (1 - there) * ROWS

    def merging(passed, finished):
        work = [
            functools.partial(one, slot, head)
            for one, slot in ((pass_on, passed), (finish, finished))
            for head in range(HEADS)
        ]
        return [[one] for one in work]

    ahead = (
        (pass_keys, 2),
        (start_kept, 3),
        (start_passed, 4),
        (pass_queries, 2),
        (start_queries, 4),
        (forward_across, 1),
    )

    def serve(now):
        for action, early in ahead:
            if isinstance(now, int):
                if 0 <= now + early < ROWS:
                    action(now + early)
            else:

                @pl.when(now + early < ROWS)
                def _():
                    action(now + early)

    for turn in range(-max(early for _, early in ahead), 1):
        serve(turn)
        if turn == -3:
            start_local()
    wait_local()
    wait_keys(0)
    wait_keys(1)
    wait_queries(0)
    attend(0, 0, 2, [[]] * 4)
    start_sides(0)

    def step(now, carry):
        serve(now)
        wait_keys(now + 1)
        wait_queries(now)

        @pl.when(now >= 2)
        def _():
            wait_sides(now - 2)

        @pl.when(now >= 4)
        def _():
            wait_home(now - 4)

        attend(now, (now - 1) * LINE, 3, merging(spare(now - 2), spare(now - 4)))
        start_sides(now)

        @pl.when(now >= 2)
        def _():
            start_home(now - 2)

        @pl.when(now >= 4)
        def _():
            stored(now - 4).start()

        return carry

    lax.fori_loop(1, ROWS - 1, step, 0)

    last = ROWS - 1
    wait_queries(last)
    wait_sides(last - 2)
    wait_home(last - 4)
    attend(last, (last - 1) * LINE, 2, merging(last - 2, last - 4))
    start_sides(last)
    start_home(last - 2)
    stored(last - 4).start()

    def pass_last(chunk):
        wait_sides(chunk)
        for head in range(HEADS):
            pass_on(chunk, head)
        start_home(chunk)

    def finish_last(chunk):
        wait_home(chunk)
        for head in range(HEADS):
            finish(chunk, head)
        stored(chunk).start()

    pass_last(last - 1)
    finish_last(last - 3)
    finish_last(last - 2)
    pass_last(last)
    finish_last(last - 1)
    finish_last(last)

    def drain(chunk, carry):
        for stream in ("kr", "kl", "vr", "vl", "kf", "vf", "qd0", "qd1"):
            copy(stream, chunk).wait_send()
        each_half(
            sends_other,
            lambda half: copy("qb", chunk, half[B]).wait_send(),
            lambda half: copy("qc", chunk, half[C]).wait_send(),
        )
        stored(chunk).wait()

        def sent(kind):
            for one in returns(kind, chunk, back[kind]):
                one.wait_send()

        sent(D)

        @pl.when(has_other)
        def _():
            sent(B)
            sent(C)

            @pl.when(has_prev)
            def _():
                sent(F)

            @pl.when(has_next)
            def _():
                copy("qf", chunk).wait_send()

        @pl.when(has_prev)
        def _():
            sent(E)

        @pl.when(has_next)
        def _():
            copy("qe", chunk).wait_send()

        return carry

    lax.fori_loop(0, ROWS, drain, 0)


def per_device(queries, key_field, value_field):
    shape = queries.shape
    flat = (FR, ROWS * LINE, HEADS * HEAD)
    args = [one.reshape(flat) for one in (queries, key_field, value_field)]
    anywhere = pl.BlockSpec(memory_space=pl.ANY)
    result = pl.pallas_call(
        kernel,
        out_shape=jax.ShapeDtypeStruct(flat, BF),
        in_specs=[anywhere] * 3,
        out_specs=anywhere,
        scratch_shapes=[
            pltpu.VMEM((4, *flat), BF),
            pltpu.VMEM((4, *flat), BF),
            pltpu.VMEM((6, *flat), BF),
            pltpu.VMEM((3, ROWS + 1, HEADS, TOK, HEAD), F32),
            pltpu.VMEM((3, ROWS + 1, HEADS, TOK, HEAD), F32),
            pltpu.VMEM((5, ROWS + 1, TOK, HEADS * HEAD), BF),
            pltpu.VMEM((5, ROWS + 1, 8, HEAD), F32),
            pltpu.VMEM((5, ROWS + 1, TOK, HEADS * HEAD), BF),
            pltpu.VMEM((5, ROWS + 1, 8, HEAD), F32),
            pltpu.SemaphoreType.DMA((5,)),
            pltpu.SemaphoreType.DMA((len(STREAMS), ROWS)),
            pltpu.SemaphoreType.DMA((len(STREAMS), ROWS)),
            pltpu.SemaphoreType.DMA((5, ROWS)),
            pltpu.SemaphoreType.DMA((5, ROWS)),
            pltpu.SemaphoreType.DMA((5, ROWS)),
            pltpu.SemaphoreType.DMA((5, ROWS)),
            pltpu.VMEM((ROWS + 1, FR, LINE, HEADS * HEAD), BF),
            pltpu.SemaphoreType.DMA((ROWS,)),
        ],
        compiler_params=pltpu.CompilerParams(
            collective_id=0, has_side_effects=True, vmem_limit_bytes=60 * 2**20
        ),
        name="tile_attention",
    )(*args)
    return result.reshape(shape)


def solution(mesh):
    spec = P(("ta", "ha"), None, "wa", None)
    return jax.shard_map(per_device, mesh=mesh, in_specs=(spec,) * 3, out_specs=spec, check_vma=False)
```

```python
import functools

import jax
import jax.numpy as jnp
from jax import lax
from jax.experimental import pallas as pl
from jax.experimental.pallas import tpu as pltpu
from jax.sharding import PartitionSpec as P

HEAD = 128
HEADS = 2
ROWS = 8
FR = 3
LINE = 64
HALF = LINE // 2
TOK = FR * LINE
FACTOR = HEAD**-0.5 * 1.4426950408889634
MESH = pl.DeviceIdType.MESH
BF = jnp.bfloat16
F32 = jnp.float32

A, D, E, B, C, F = range(6)
BLOCK = 768
STREAMS = ("kr", "kl", "vr", "vl", "kf", "vf", "qb", "qc", "qd0", "qd1", "qe", "qf")
RETURNS = {B: 0, C: 1, D: 2, E: 3, F: 4}
LOCAL = {A: 0, D: 1, C: 2}


def rows_of(chunk):
    return pl.ds(pl.multiple_of(chunk * LINE, LINE), LINE)


def merge(parts):
    top = functools.reduce(jnp.maximum, [log for _, log in parts])
    shares = [jnp.exp2(log - top) for _, log in parts]
    total = functools.reduce(jnp.add, shares)
    value = functools.reduce(jnp.add, [share * out for share, (out, _) in zip(shares, parts)])
    return value / total, top + jnp.log2(total)


def kernel(
    q_in, k_in, v_in, out, kbuf, vbuf, qbuf, okeep, lkeep, osend, lsend, orecv, lrecv, local_sem, send_sem, recv_sem,
    osend_sem, orecv_sem, lsend_sem, lrecv_sem, done, out_sem
):
    core = lax.axis_index("ta")
    ha = lax.axis_index("ha")
    wa = lax.axis_index("wa")
    z, x_lo, y, x_hi = ha % 4, ha // 4, wa // 2, wa % 2
    zt = z // 2

    def device(lo, hi, yy, zz, cc):
        return {"ta": cc, "ha": lo * 4 + zz, "wa": yy * 2 + hi}

    swap = 1 - (x_lo + zt) % 2
    out_core = (core + swap) % 2
    in_core = (core + 1 - swap) % 2
    has_other = (swap == 1) | (core == zt)
    sends_other = (swap == 0) | (core != zt)
    right = device(x_lo, x_hi, y, (z + 1) % 4, core)
    left = device(x_lo, x_hi, y, (z + 3) % 4, core)
    step_y = 1 - 2 * x_hi
    y_next = device(x_lo, x_hi, (y + step_y + 4) % 4, z, core)
    y_prev = device(x_lo, x_hi, (y - step_y + 4) % 4, z, core)
    y_first = 3 * x_hi
    has_prev = y != y_first
    has_next = y != 3 - y_first
    near_out = device(1 - x_lo, x_hi, y, z, out_core)
    near_in = device(1 - x_lo, x_hi, y, z, in_core)
    diag_out = device(1 - x_lo, 1 - x_hi, y, z, out_core)
    diag_in = device(1 - x_lo, 1 - x_hi, y, z, in_core)
    across = device(x_lo, 1 - x_hi, y, z, core)

    barrier = pltpu.get_barrier_semaphore()
    peers = (right, left, y_next, y_prev, near_out, near_in, diag_out, diag_in, across)
    for peer in peers:
        pl.semaphore_signal(barrier, inc=1, device_id=peer, device_id_type=MESH)
    pl.semaphore_wait(barrier, len(peers))

    def remote(stream, chunk, src, dst, target):
        at = STREAMS.index(stream)
        return pltpu.make_async_remote_copy(
            src_ref=src, dst_ref=dst, send_sem=send_sem.at[at, chunk], recv_sem=recv_sem.at[at, chunk],
            device_id=target, device_id_type=MESH
        )

    def part(ref, *lead, chunk, half=None):
        rows = rows_of(chunk) if half is None else pl.ds(pl.multiple_of(chunk * LINE + half * HALF, HALF), HALF)
        return ref.at[(*lead, slice(None), rows, slice(None))]

    def copy(stream, chunk, half=None):
        if stream in ("kr", "kl"):
            return remote(stream, chunk, part(k_in, chunk=chunk), part(kbuf, z, chunk=chunk), right if stream == "kr" else left)
        if stream in ("vr", "vl"):
            return remote(stream, chunk, part(v_in, chunk=chunk), part(vbuf, z, chunk=chunk), right if stream == "vr" else left)
        if stream == "kf":
            slab = (z + 3) % 4
            return remote(stream, chunk, part(kbuf, slab, chunk=chunk), part(kbuf, slab, chunk=chunk), right)
        if stream == "vf":
            slab = (z + 1) % 4
            return remote(stream, chunk, part(vbuf, slab, chunk=chunk), part(vbuf, slab, chunk=chunk), left)
        if stream == "qb":
            return remote(stream, chunk, part(q_in, chunk=chunk, half=half), part(qbuf, B, chunk=chunk, half=half), near_out)
        if stream == "qc":
            return remote(stream, chunk, part(q_in, chunk=chunk, half=half), part(qbuf, C, chunk=chunk, half=half), diag_out)
        if stream == "qd0":
            return remote(stream, chunk, part(qbuf, B, chunk=chunk, half=0), part(qbuf, D, chunk=chunk, half=0), diag_in)
        if stream == "qd1":
            return remote(stream, chunk, part(qbuf, C, chunk=chunk, half=1), part(qbuf, D, chunk=chunk, half=1), near_in)
        if stream == "qe":
            return remote(stream, chunk, part(qbuf, D, chunk=chunk), part(qbuf, E, chunk=chunk), y_next)
        return remote(stream, chunk, part(qbuf, C, chunk=chunk), part(qbuf, F, chunk=chunk), y_next)

    def arrival(stream, chunk, half=None):
        if stream in ("kr", "kl", "kf"):
            slab = (z + {"kr": 3, "kl": 1, "kf": 2}[stream]) % 4
            ref = part(kbuf, slab, chunk=chunk)
        elif stream in ("vr", "vl", "vf"):
            slab = (z + {"vr": 3, "vl": 1, "vf": 2}[stream]) % 4
            ref = part(vbuf, slab, chunk=chunk)
        elif stream == "qd0":
            ref = part(qbuf, D, chunk=chunk, half=0)
        elif stream == "qd1":
            ref = part(qbuf, D, chunk=chunk, half=1)
        else:
            ref = part(qbuf, {"qb": B, "qc": C, "qe": E, "qf": F}[stream], chunk=chunk, half=half)
        return remote(stream, chunk, ref, ref, right)

    def returns(kind, chunk, target):
        at = RETURNS[kind]
        return (
            pltpu.make_async_remote_copy(
                src_ref=osend.at[at, chunk], dst_ref=orecv.at[at, chunk], send_sem=osend_sem.at[at, chunk],
                recv_sem=orecv_sem.at[at, chunk], device_id=target, device_id_type=MESH
            ),
            pltpu.make_async_remote_copy(
                src_ref=lsend.at[at, chunk], dst_ref=lrecv.at[at, chunk], send_sem=lsend_sem.at[at, chunk],
                recv_sem=lrecv_sem.at[at, chunk], device_id=target, device_id_type=MESH
            ),
        )

    back = {B: near_in, C: diag_in, D: across, E: y_prev, F: y_prev}

    only = {B: 0, C: 1}

    def each_half(whole, *actions):
        @pl.when(whole)
        def _():
            for action in actions:
                action({B: None, C: None})

        @pl.when(jnp.logical_not(whole))
        def _():
            for action in actions:
                action(only)

    lane = lax.broadcasted_iota(jnp.int32, (HEAD, HEAD), 1)
    eye = lane == lax.broadcasted_iota(jnp.int32, (HEAD, HEAD), 0)

    def put_back(kind, slot, head, value, log):
        at = RETURNS[kind]
        osend[at, slot, :, head * HEAD : (head + 1) * HEAD] = value.astype(BF)
        for half, (begin, size) in enumerate(((0, HEAD), (HEAD, TOK - HEAD))):
            picked = jnp.where(eye[:size], log[begin : begin + size], 0.0)
            row = 2 * head + half
            lsend[at, slot, row : row + 1, :] = jnp.sum(picked, axis=0, keepdims=True)

    def came_back(kind, slot, head):
        at = RETURNS[kind]
        logs = []
        for half, size in enumerate((HEAD, TOK - HEAD)):
            row = 2 * head + half
            spread = jnp.broadcast_to(lrecv[at, slot, row : row + 1, :], (size, HEAD))
            logs.append(jnp.sum(jnp.where(eye[:size], spread, 0.0), axis=1, keepdims=True))
        log = jnp.broadcast_to(jnp.concatenate(logs, axis=0), (TOK, HEAD))
        return orecv[at, slot, :, head * HEAD : (head + 1) * HEAD].astype(F32), log

    def kept(kind, slot, head):
        return okeep[LOCAL[kind], slot, head], lkeep[LOCAL[kind], slot, head]

    def pass_on(slot, head):
        for kind, extra in ((D, E), (C, F)):
            put_back(kind, slot, head, *merge([kept(kind, slot, head), came_back(extra, slot, head)]))

    def finish(slot, head):
        parts = [kept(A, slot, head)] + [came_back(kind, slot, head) for kind in (D, B, C)]
        value, _ = merge(parts)
        done[slot, :, :, head * HEAD : (head + 1) * HEAD] = value.astype(BF).reshape(FR, LINE, HEAD)

    def attend(chunk, begin, span, extras):
        keys = pl.ds(pl.multiple_of(begin, LINE), span * LINE)
        groups = (((A, D, E), (0, 1, 2, 3)), ((B, C, F), (2 - 2 * zt, 3 - 2 * zt)))
        jobs = [(sets, slabs, head) for sets, slabs in groups for head in range(HEADS)]

        def pieces(ref, slabs, lanes):
            whole = jnp.concatenate(
                [ref[slab, :, keys, lanes].reshape(FR * span * LINE, HEAD) for slab in slabs], axis=0
            )
            return [whole[at : at + BLOCK] for at in range(0, whole.shape[0], BLOCK)]

        def products(job):
            sets, slabs, head = job
            lanes = pl.ds(head * HEAD, HEAD)
            queries = qbuf[sets[0] : sets[0] + 3, :, rows_of(chunk), lanes].reshape(3 * TOK, HEAD)
            return [
                lax.dot_general(queries, piece, (((1,), (1,)), ((), ())), preferred_element_type=F32)
                for piece in pieces(kbuf, slabs, lanes)
            ]

        scores = products(jobs[0])
        for number, (sets, slabs, head) in enumerate(jobs):
            later = products(jobs[number + 1]) if number + 1 < len(jobs) else None
            columns = [one[:, at : at + HEAD] for one in scores for at in range(0, one.shape[1], HEAD)]
            top = jnp.max(functools.reduce(jnp.maximum, columns), axis=1, keepdims=True) * FACTOR
            summed = None
            for one, piece in zip(scores, pieces(vbuf, slabs, pl.ds(head * HEAD, HEAD))):
                weights = jnp.exp2(one * FACTOR - top).astype(BF)
                product = jnp.dot(
                    weights, jnp.concatenate([piece, jnp.ones_like(piece)], axis=1), preferred_element_type=F32
                )
                summed = product if summed is None else summed + product
            totals = summed[:, HEAD:]
            mean = summed[:, :HEAD] / totals
            logs = top + jnp.log2(totals)
            for at, kind in enumerate(sets):
                value, log = mean[at * TOK : (at + 1) * TOK], logs[at * TOK : (at + 1) * TOK]
                if kind in LOCAL:
                    okeep[LOCAL[kind], chunk, head], lkeep[LOCAL[kind], chunk, head] = value, log
                else:
                    put_back(kind, chunk, head, value, log)
            scores = later
            for extra in extras[number]:
                extra()

    def start_back(kind, chunk):
        for one in returns(kind, chunk, back[kind]):
            one.start()

    def wait_back(kind, chunk):
        for one in returns(kind, chunk, back[kind]):
            one.wait_recv()

    own = [
        pltpu.make_async_copy(k_in, kbuf.at[z], local_sem.at[0]),
        pltpu.make_async_copy(v_in, vbuf.at[z], local_sem.at[1]),
        pltpu.make_async_copy(q_in, qbuf.at[A], local_sem.at[2]),
    ]
    def start_local():
        for one in own:
            one.start()
        fill_absent()

    def wait_local():
        for one in own:
            one.wait()

    def fill_absent():
        @pl.when(jnp.logical_not(has_prev))
        def _():
            fill = pltpu.make_async_copy(q_in, qbuf.at[E], local_sem.at[3])
            fill.start()
            fill.wait()

        @pl.when(jnp.logical_not(has_prev & has_other))
        def _():
            fill = pltpu.make_async_copy(q_in, qbuf.at[F], local_sem.at[4])
            fill.start()
            fill.wait()

        def absent(kind):
            def blank(slot, carry):
                orecv[RETURNS[kind], slot] = jnp.zeros((TOK, HEADS * HEAD), BF)
                lrecv[RETURNS[kind], slot] = jnp.full((8, HEAD), -1e30, F32)
                return carry

            lax.fori_loop(0, ROWS, blank, 0)

        @pl.when(jnp.logical_not(has_next))
        def _():
            absent(E)

        @pl.when(jnp.logical_not(has_next & has_other))
        def _():
            absent(F)

        @pl.when(jnp.logical_not(sends_other))
        def _():
            absent(B)
            absent(C)

    def start_kept(chunk):
        copy("kl", chunk).start()
        copy("vr", chunk).start()

    def start_passed(chunk):
        copy("kr", chunk).start()
        copy("vl", chunk).start()

    def pass_keys(chunk):
        arrival("kr", chunk).wait_recv()
        copy("kf", chunk).start()
        arrival("vl", chunk).wait_recv()
        copy("vf", chunk).start()

    def start_queries(chunk):
        each_half(
            sends_other,
            lambda half: copy("qb", chunk, half[B]).start(),
            lambda half: copy("qc", chunk, half[C]).start(),
        )

    def pass_queries(chunk):
        each_half(
            has_other,
            lambda half: arrival("qb", chunk, half[B]).wait_recv(),
            lambda half: arrival("qc", chunk, half[C]).wait_recv(),
        )
        copy("qd0", chunk).start()
        copy("qd1", chunk).start()

    def forward_across(chunk):
        arrival("qd0", chunk).wait_recv()
        arrival("qd1", chunk).wait_recv()

        @pl.when(has_next)
        def _():
            copy("qe", chunk).start()

            @pl.when(has_other)
            def _():
                copy("qf", chunk).start()

    def wait_keys(chunk):
        for stream in ("kl", "vr", "kf", "vf"):
            arrival(stream, chunk).wait_recv()

    def wait_queries(chunk):
        @pl.when(has_prev)
        def _():
            arrival("qe", chunk).wait_recv()

            @pl.when(has_other)
            def _():
                arrival("qf", chunk).wait_recv()

    def wait_sides(chunk):
        @pl.when(has_next)
        def _():
            wait_back(E, chunk)

            @pl.when(has_other)
            def _():
                wait_back(F, chunk)

    def wait_home(chunk):
        wait_back(D, chunk)

        @pl.when(sends_other)
        def _():
            wait_back(B, chunk)
            wait_back(C, chunk)

    def start_sides(chunk):
        @pl.when(has_prev)
        def _():
            start_back(E, chunk)

            @pl.when(has_other)
            def _():
                start_back(F, chunk)

        @pl.when(has_other)
        def _():
            start_back(B, chunk)

    def start_home(chunk):
        start_back(D, chunk)

        @pl.when(has_other)
        def _():
            start_back(C, chunk)

    def stored(chunk):
        return pltpu.make_async_copy(done.at[chunk], out.at[:, rows_of(chunk), :], out_sem.at[chunk])

    def spare(chunk):
        there = (chunk + ROWS) // ROWS
        return there * chunk + (1 - there) * ROWS

    def merging(passed, finished):
        work = [
            functools.partial(one, slot, head)
            for one, slot in ((pass_on, passed), (finish, finished))
            for head in range(HEADS)
        ]
        return [[one] for one in work]

    ahead = (
        (start_queries, 4),
        (pass_keys, 2),
        (start_kept, 3),
        (start_passed, 4),
        (pass_queries, 2),
        (forward_across, 1),
    )

    def serve(now):
        for action, early in ahead:
            if isinstance(now, int):
                if 0 <= now + early < ROWS:
                    action(now + early)
            else:

                @pl.when(now + early < ROWS)
                def _():
                    action(now + early)

    for turn in range(-max(early for _, early in ahead), 1):
        serve(turn)
        if turn == -3:
            start_local()
    wait_local()
    wait_keys(0)
    wait_keys(1)
    wait_queries(0)
    attend(0, 0, 2, [[]] * 4)
    start_sides(0)

    def step(now, carry):
        serve(now)
        wait_keys(now + 1)
        wait_queries(now)

        @pl.when(now >= 2)
        def _():
            wait_sides(now - 2)

        @pl.when(now >= 4)
        def _():
            wait_home(now - 4)

        attend(now, (now - 1) * LINE, 3, merging(spare(now - 2), spare(now - 4)))
        start_sides(now)

        @pl.when(now >= 2)
        def _():
            start_home(now - 2)

        @pl.when(now >= 4)
        def _():
            stored(now - 4).start()

        return carry

    lax.fori_loop(1, ROWS - 1, step, 0)

    last = ROWS - 1
    wait_queries(last)
    wait_sides(last - 2)
    wait_home(last - 4)
    attend(last, (last - 1) * LINE, 2, merging(last - 2, last - 4))
    start_sides(last)
    start_home(last - 2)
    stored(last - 4).start()

    def pass_last(chunk):
        wait_sides(chunk)
        for head in range(HEADS):
            pass_on(chunk, head)
        start_home(chunk)

    def finish_last(chunk):
        wait_home(chunk)
        for head in range(HEADS):
            finish(chunk, head)
        stored(chunk).start()

    pass_last(last - 1)
    finish_last(last - 3)
    finish_last(last - 2)
    pass_last(last)
    finish_last(last - 1)
    finish_last(last)

    def drain(chunk, carry):
        for stream in ("kr", "kl", "vr", "vl", "kf", "vf", "qd0", "qd1"):
            copy(stream, chunk).wait_send()
        each_half(
            sends_other,
            lambda half: copy("qb", chunk, half[B]).wait_send(),
            lambda half: copy("qc", chunk, half[C]).wait_send(),
        )
        stored(chunk).wait()

        def sent(kind):
            for one in returns(kind, chunk, back[kind]):
                one.wait_send()

        sent(D)

        @pl.when(has_other)
        def _():
            sent(B)
            sent(C)

            @pl.when(has_prev)
            def _():
                sent(F)

            @pl.when(has_next)
            def _():
                copy("qf", chunk).wait_send()

        @pl.when(has_prev)
        def _():
            sent(E)

        @pl.when(has_next)
        def _():
            copy("qe", chunk).wait_send()

        return carry

    lax.fori_loop(0, ROWS, drain, 0)


def per_device(queries, key_field, value_field):
    shape = queries.shape
    flat = (FR, ROWS * LINE, HEADS * HEAD)
    args = [one.reshape(flat) for one in (queries, key_field, value_field)]
    anywhere = pl.BlockSpec(memory_space=pl.ANY)
    result = pl.pallas_call(
        kernel,
        out_shape=jax.ShapeDtypeStruct(flat, BF),
        in_specs=[anywhere] * 3,
        out_specs=anywhere,
        scratch_shapes=[
            pltpu.VMEM((4, *flat), BF),
            pltpu.VMEM((4, *flat), BF),
            pltpu.VMEM((6, *flat), BF),
            pltpu.VMEM((3, ROWS + 1, HEADS, TOK, HEAD), F32),
            pltpu.VMEM((3, ROWS + 1, HEADS, TOK, HEAD), F32),
            pltpu.VMEM((5, ROWS + 1, TOK, HEADS * HEAD), BF),
            pltpu.VMEM((5, ROWS + 1, 8, HEAD), F32),
            pltpu.VMEM((5, ROWS + 1, TOK, HEADS * HEAD), BF),
            pltpu.VMEM((5, ROWS + 1, 8, HEAD), F32),
            pltpu.SemaphoreType.DMA((5,)),
            pltpu.SemaphoreType.DMA((len(STREAMS), ROWS)),
            pltpu.SemaphoreType.DMA((len(STREAMS), ROWS)),
            pltpu.SemaphoreType.DMA((5, ROWS)),
            pltpu.SemaphoreType.DMA((5, ROWS)),
            pltpu.SemaphoreType.DMA((5, ROWS)),
            pltpu.SemaphoreType.DMA((5, ROWS)),
            pltpu.VMEM((ROWS + 1, FR, LINE, HEADS * HEAD), BF),
            pltpu.SemaphoreType.DMA((ROWS,)),
        ],
        compiler_params=pltpu.CompilerParams(
            collective_id=0, has_side_effects=True, vmem_limit_bytes=60 * 2**20
        ),
        name="tile_attention",
    )(*args)
    return result.reshape(shape)


def solution(mesh):
    spec = P(("ta", "ha"), None, "wa", None)
    return jax.shard_map(per_device, mesh=mesh, in_specs=(spec,) * 3, out_specs=spec, check_vma=False)
```
